32 devices in a mesh: node: 4 (over y, core), seq: 8 (over z, x).
Axes of the slice: x: 2, y: 2, z: 4, core: 2. Of those that a mesh axis runs over, the one named last changes fastest.
Arguments:
- queries: bfloat16 [4096, 4096], P(('node', 'seq')), may hold values from -21 to 21
- keys: bfloat16 [4096, 1024], P(('node', 'seq')), may hold values from -6 to 6
- values: bfloat16 [4096, 1024], P(('node', 'seq')), may hold values from -12 to 12
- routes: int32 [4096, 4], P(('node', 'seq')), may hold values from 0 to 7, all different within a row; in each aligned block of 128 rows (0 to 127, 128 to 255, ...) at most 96 rows name the same one
- gates: bfloat16 [4096, 4], P(('node', 'seq')), may hold values from 0.099609375 to 0.59765625
Outputs:
- expert_rows: bfloat16 [8, 8, 4, 96, 4096], P('node', 'seq')
The draws below stay inside these ranges and needn't reach their ends.
Inputs may be any that keep to these rules, and one draw needn't show every extreme that they name: `routes`: each row names 4 different experts. In the rows of one device (128 rows, aligned) no expert is named by more than 96 rows, a bound that some block reaches.
All inputs are finite; a program needn't handle non-finite values.
Results may differ from the reference program's by a relative error of at most 0.0057.
Values may be sent and summed in bfloat16 or wider, within the bound.
A program may use at most 64 MiB of HBM per device.

```python
import math
import jax
import jax.numpy as jnp
import numpy as np
from jax import lax

QUERY_HEADS = 32
KEY_VALUE_HEADS = 8
HEAD_SIZE = 128
TOP = 4
TOK_DEV = 128
EXPERTS = 8
CAP = 96
TOKEN_TOTAL = 4096
N_NODE = 4
N_SEQ = 8


def common_sample(key, width):
    gaussian_noise = jax.random.normal(key, (TOKEN_TOTAL, width), jnp.float32)
    return gaussian_noise


def draw_keys(key, part):
    gaussian_noise = common_sample(key, KEY_VALUE_HEADS * HEAD_SIZE)
    return jnp.clip(1.5 * gaussian_noise, -6.0, 6.0).astype(jnp.bfloat16)


def draw_queries(key, part):
    key = jax.random.fold_in(key, 3)
    return jnp.clip(1.5 * jax.random.normal(key, (TOKEN_TOTAL, QUERY_HEADS * HEAD_SIZE), jnp.float32), -6.0, 6.0).astype(jnp.bfloat16)


def level_of(rng, dims, pieces, least, high):
    def one(axis_at, shards_of):
        draws = jax.random.uniform(jax.random.fold_in(jax.random.fold_in(rng, 6), axis_at), (shards_of,), jnp.float32, least / len(pieces), high / len(pieces))
        return jnp.repeat(jnp.exp(draws), dims[axis_at] // shards_of).reshape((-1,) + (1,) * (len(dims) - axis_at - 1))

    level = one(*pieces[0])
    for cut in pieces[1:]:
        level = level * one(*cut)
    return level


def deal_out(rng, own, number, rows, count, top, limit, slope):
    order = jax.random.permutation(rng, count)
    heavy_load, ordinary = portions_of(count, rows * top, limit, slope, True), portions_of(count, rows * top, limit, slope, False)
    places = jnp.arange(count)

    def named(tallies, rotation):
        used = int((tallies > 0).sum())
        fixed = max(1, used // 4)
        moved = fixed + (places - fixed + rotation * (used - fixed)) % max(1, count - fixed)
        return jnp.zeros((count,), jnp.int32).at[order[jnp.where(places < fixed, places, moved)]].set(jnp.asarray(tallies, jnp.int32))

    tallies = jnp.where(number % 4 == 0, named(heavy_load, number // 4), named(ordinary, number - number // 4 - 1))
    mixed = jax.random.permutation(jax.random.fold_in(own, 3), count)
    source_of, sink = mixed[0:count // 2 * 2:2], mixed[1:count // 2 * 2:2]
    slack = jnp.minimum(tallies[source_of] - 1, limit - tallies[sink]) // 2
    slack = jnp.where((source_of == order[0]) | (sink == order[0]) | (tallies[sink] == 0), 0, jnp.maximum(slack, 0))
    moved = jax.random.randint(jax.random.fold_in(own, 4), (count // 2,), 0, 1 << 20) % (slack + 1)
    tallies = tallies.at[source_of].add(-moved).at[sink].add(moved)
    members = jnp.searchsorted(jnp.cumsum(tallies), jnp.arange(rows * top), side="right").astype(jnp.int32)
    listing = members.reshape(top, rows).T
    listing = listing[jax.random.permutation(jax.random.fold_in(own, 1), rows)]
    rotation = jax.random.randint(jax.random.fold_in(own, 2), (rows, 1), 0, top)
    return jnp.take_along_axis(listing, (jnp.arange(top)[None, :] + rotation) % top, axis=1)


def portions_of(number_of, total, limit, slope, full):
    portions = [(1 << 20) // math.isqrt(standing ** slope) + 1 for standing in range(1, number_of + 1)]
    largest = limit if full else min(limit, max(-(-total // number_of), total * portions[0] // sum(portions)))
    least = 1 if total - largest >= number_of - 1 else 0
    holding, surplus = [largest] + [least] * (number_of - 1), total - largest - least * (number_of - 1)
    while surplus > 0:
        movable = [i for i in range(1, number_of) if holding[i] < largest] or [i for i in range(1, number_of) if holding[i] < limit]
        pool, remaining = sum([portions[i] for i in movable]), surplus
        for i in movable:
            more = min(limit - holding[i], max(1, remaining * portions[i] // pool), surplus)
            holding[i] = holding[i] + more
            surplus = surplus - more
    return np.array(holding)


def normal_values(rng, dims, spread, most, split=(), held_as=jnp.bfloat16):
    factor_of = level_of(rng, dims, split, -0.22, 0.18) if split else 1.0
    result = jax.random.normal(rng, dims, jnp.float32) * spread * factor_of
    return jnp.minimum(jnp.maximum(result, -most), most).astype(held_as)


def setup_inputs(seed: int = 0) -> dict:
    key_list = jax.random.split(jax.random.key(seed), 6)
    queries = draw_queries(jax.random.fold_in(key_list[5], 71), 0)
    keys = draw_keys(jax.random.fold_in(key_list[5], 71), 0)
    values = normal_values(key_list[2], (TOKEN_TOTAL, KEY_VALUE_HEADS * HEAD_SIZE), 3.0, 12.0, ((0, 32),))
    routes_keys = jax.random.split(jax.random.fold_in(key_list[3], 1), TOKEN_TOTAL // TOK_DEV)
    routes_turns = jax.random.permutation(jax.random.fold_in(key_list[3], 3), TOKEN_TOTAL // TOK_DEV)
    routes = jax.vmap(lambda own, number: deal_out(jax.random.fold_in(key_list[3], 2), own, number, TOK_DEV, EXPERTS, TOP, CAP, 2))(routes_keys, routes_turns).reshape((TOKEN_TOTAL, TOP))
    gates = jnp.clip(0.099609375 + 0.49804688 * jax.random.uniform(key_list[4], (TOKEN_TOTAL, TOP), jnp.float32) ** level_of(key_list[4], (TOKEN_TOTAL, TOP), ((0, 32),), -0.2, 0.2), 0.099609375, 0.59765625).astype(jnp.bfloat16)
    return {"queries": queries, "keys": keys, "values": values, "routes": routes, "gates": gates}


def head_attention(q_head, k_head, v_head, span_rows):
    span_length = q_head.shape[0]
    score_scale = q_head.shape[1] ** -0.5
    key_pos = jnp.arange(span_length, dtype=jnp.int32)

    def one_span(begin_row):
        q_span = lax.dynamic_slice_in_dim(q_head, begin_row, span_rows, 0)
        scores = jnp.dot(q_span, k_head.T, preferred_element_type=jnp.float32) * score_scale
        query_pos = begin_row + jnp.arange(span_rows, dtype=jnp.int32)
        scores = jnp.where(key_pos[None, :] <= query_pos[:, None], scores, jnp.float32(-1e30))
        top_score = jnp.max(scores, axis=1, keepdims=True)
        raised = jnp.exp(scores - top_score)
        shares = (raised / jnp.sum(raised, axis=1, keepdims=True)).astype(jnp.bfloat16)
        return jnp.dot(shares, v_head, preferred_element_type=jnp.float32).astype(jnp.bfloat16)

    begins = jnp.arange(span_length // span_rows, dtype=jnp.int32) * span_rows
    return lax.map(one_span, begins).reshape(span_length, -1)


def reference(queries, keys, values, routes, gates):
    span_length = TOK_DEV * N_SEQ
    group_members = QUERY_HEADS // KEY_VALUE_HEADS
    span_rows = min(512, span_length)
    q_all = queries.reshape(N_NODE, span_length, QUERY_HEADS, HEAD_SIZE)
    key_stack = keys.reshape(N_NODE, span_length, KEY_VALUE_HEADS, HEAD_SIZE)
    value_stack = values.reshape(N_NODE, span_length, KEY_VALUE_HEADS, HEAD_SIZE)

    def one_head(flat_index):
        seq_no = flat_index // QUERY_HEADS
        head_no = flat_index % QUERY_HEADS
        kv_no = head_no // group_members
        return head_attention(q_all[seq_no, :, head_no, :], key_stack[seq_no, :, kv_no, :], value_stack[seq_no, :, kv_no, :], span_rows)

    head_out = lax.map(one_head, jnp.arange(N_NODE * QUERY_HEADS, dtype=jnp.int32))
    attended = head_out.reshape(N_NODE, QUERY_HEADS, span_length, HEAD_SIZE).transpose(0, 2, 1, 3).reshape(N_NODE * N_SEQ, TOK_DEV, QUERY_HEADS * HEAD_SIZE)

    dev_routes = routes.reshape(N_NODE * N_SEQ, TOK_DEV, TOP)
    dev_gates = gates.astype(jnp.float32).reshape(N_NODE * N_SEQ, TOK_DEV, TOP)
    slot_ids = jnp.arange(CAP, dtype=jnp.int32)
    tok_ids = jnp.arange(TOK_DEV, dtype=jnp.int32)
    source_ids = jnp.arange(N_NODE * N_SEQ, dtype=jnp.int32)[:, None]

    def one_expert(expert):
        match = dev_routes == expert
        member = jnp.sum(match.astype(jnp.int32), axis=2)
        weight = jnp.sum(jnp.where(match, dev_gates, jnp.float32(0.0)), axis=2)
        ranked = jnp.cumsum(member, axis=1) - member
        picked = (member[:, None, :] == 1) & (ranked[:, None, :] == slot_ids[None, :, None])
        filled = jnp.sum(picked.astype(jnp.int32), axis=2)
        where_tok = jnp.sum(jnp.where(picked, tok_ids[None, None, :], 0), axis=2).astype(jnp.int32)
        chosen = attended[source_ids, where_tok].astype(jnp.float32)
        slot_gate = weight[source_ids, where_tok]
        dispatched = jnp.where(filled[:, :, None] == 1, slot_gate[:, :, None] * chosen, jnp.float32(0.0)).astype(jnp.bfloat16)
        return dispatched.reshape(N_NODE, N_SEQ, CAP, QUERY_HEADS * HEAD_SIZE).transpose(1, 0, 2, 3)

    return lax.map(one_expert, jnp.arange(EXPERTS, dtype=jnp.int32))
```

```python
import functools

import jax
import jax.numpy as jnp
from jax import lax
from jax.experimental import pallas as pl
from jax.experimental.pallas import tpu as pltpu
from jax.sharding import PartitionSpec as P

QUERY_HEADS = 32
KEY_VALUE_HEADS = 8
HEAD_SIZE = 128
TOP = 4
EXP_NODE = 2
MEMBERS = QUERY_HEADS // KEY_VALUE_HEADS
GROUP_COLS = MEMBERS * HEAD_SIZE
LOG2E = 1.4426950408889634
MESH = pl.DeviceIdType.MESH


def attend_kernel(
    n_node, n_seq, rows,
    q_ref, wt_ref, k_hbm, v_hbm, all_hbm, wts_hbm,
    kv, att, kv_local, kv_recv, z_send, x_send,
    a_local, a_recv, a_core, a_far, a_fwd, w_local, w_recv, w_send,
):
    n = lax.axis_index("node")
    s = lax.axis_index("seq")
    a, b = s // 2, lax.rem(s, 2)
    depth = n_seq // 2
    far = n_node // 2
    y, core = n // 2, lax.rem(n, 2)
    mate = 2 * y + 1 - core
    beside = 2 * a + 1 - b
    groups = KEY_VALUE_HEADS

    def remote(src, dst, send, recv, node, seq):
        return pltpu.make_async_remote_copy(
            src_ref=src, dst_ref=dst, send_sem=send, recv_sem=recv,
            device_id=(node, seq), device_id_type=MESH,
        )

    def own_copy(c, which):
        src = (k_hbm, v_hbm)[which].at[:, pl.ds(pl.multiple_of(c * HEAD_SIZE, HEAD_SIZE), HEAD_SIZE)]
        dst = kv.at[c, which, pl.ds(pl.multiple_of(s * rows, rows), rows), :]
        return pltpu.make_async_copy(src, dst, kv_local.at[c, which])

    def block(c, j):
        return kv.at[c, :, pl.ds(pl.multiple_of(j * rows, rows), rows), :]

    def z_copy(c, line):
        ref = block(c, 2 * line + b)
        return remote(ref, ref, z_send.at[c, line], kv_recv.at[c, 2 * line + b], n, s + 2)

    def x_copy(c, line):
        ref = block(c, 2 * line + b)
        return remote(ref, ref, x_send.at[c, line], kv_recv.at[c, 2 * line + b], n, beside)

    def kv_arrived(c, j):
        ref = block(c, j)
        remote(ref, ref, z_send.at[c, 0], kv_recv.at[c, j], n, beside).wait_recv()

    def loop(body):
        def step(c, carry):
            body(c)
            return carry
        lax.fori_loop(0, groups, step, 0)

    def load(c):
        own_copy(c, 0).start()
        own_copy(c, 1).start()

    loop(load)

    barrier = pltpu.get_barrier_semaphore()

    def greet(node, seq):
        pl.semaphore_signal(barrier, inc=1, device_id=(node, seq), device_id_type=MESH)

    greet(n, beside)
    for k in range(1, n_node):
        greet(lax.rem(n + k, n_node), s)

    @pl.when(a > 0)
    def _():
        greet(n, s - 2)

    @pl.when(a < depth - 1)
    def _():
        greet(n, s + 2)

    edges = (a > 0).astype(jnp.int32) + (a < depth - 1).astype(jnp.int32)
    pl.semaphore_wait(barrier, n_node + edges)

    def pass_on(c, line, own):
        @pl.when(a < depth - 1)
        def _():
            z_copy(c, line).start()

        if own:
            @pl.when(b == 0)
            def _():
                x_copy(c, line).start()
        else:
            x_copy(c, line).start()

    def own_out(c):
        own_copy(c, 0).wait()
        own_copy(c, 1).wait()
        pass_on(c, a, True)

    def forward(c):
        for lag in range(1, depth):
            @pl.when(lag <= a)
            def _():
                line = a - lag
                kv_arrived(c, 2 * line + b)
                pass_on(c, line, False)

    def x_arrivals(c):
        @pl.when(b == 1)
        def _():
            kv_arrived(c, 2 * a)

        for lag in range(1, depth):
            @pl.when(lag <= a)
            def _():
                kv_arrived(c, 2 * (a - lag) + 1 - b)

    def wide(c):
        return pl.ds(pl.multiple_of(c * GROUP_COLS, GROUP_COLS), GROUP_COLS)

    def landing(c, node):
        return all_hbm.at[node, :, wide(c)]

    def att_local(c):
        return pltpu.make_async_copy(att.at[:, wide(c)], landing(c, n), a_local.at[c])

    def att_core(c):
        return remote(att.at[:, wide(c)], landing(c, n), a_core.at[c], a_recv.at[c, n], mate, s)

    def att_far(c, k):
        other = 2 * lax.rem(y + k, far) + core
        return remote(att.at[:, wide(c)], landing(c, n), a_far.at[c, k], a_recv.at[c, n], other, s)

    def att_fwd(c, k):
        origin = 2 * lax.rem(y + k, far) + core
        ref = landing(c, origin)
        return remote(ref, ref, a_fwd.at[c, k], a_recv.at[c, origin], mate, s)

    def att_arrived(c, node):
        ref = landing(c, node)
        remote(ref, ref, a_core.at[c], a_recv.at[c, node], mate, s).wait_recv()

    def att_forward(c):
        for k in range(1, far):
            att_arrived(c, 2 * lax.rem(y + k, far) + core)
            att_fwd(c, k).start()

    span = n_seq * rows
    query_pos = s * rows + lax.broadcasted_iota(jnp.int32, (rows, span), 0)
    allowed = lax.broadcasted_iota(jnp.int32, (rows, span), 1) <= query_pos

    def compute(c):
        k_part = kv[c, 0]
        v_part = kv[c, 1]
        for h in range(MEMBERS):
            cols = pl.ds(pl.multiple_of(c * GROUP_COLS + h * HEAD_SIZE, HEAD_SIZE), HEAD_SIZE)
            scores = lax.dot_general(
                q_ref[:, cols], k_part, (((1,), (1,)), ((), ())),
                preferred_element_type=jnp.float32,
            )
            scores = jnp.where(allowed, scores, jnp.float32(-1e30))
            top = jnp.max(scores, axis=1, keepdims=True)
            raised = jnp.exp2((scores - top) * jnp.float32(HEAD_SIZE ** -0.5 * LOG2E))
            total = jnp.sum(raised, axis=1, keepdims=True)
            shares = (raised * (1.0 / total)).astype(jnp.bfloat16)
            att[:, cols] = jnp.dot(
                shares, v_part, preferred_element_type=jnp.float32
            ).astype(jnp.bfloat16)

    def send_att(c):
        for k in range(1, far):
            att_far(c, k).start()
        att_core(c).start()
        att_local(c).start()

    def w_copy(k):
        other = lax.rem(n + k, n_node)
        return remote(wt_ref, wts_hbm.at[n], w_send.at[k], w_recv.at[n], other, s)

    own_out(0)
    own_out(1)

    pltpu.make_async_copy(wt_ref, wts_hbm.at[n], w_local).start()
    for k in range(1, n_node):
        w_copy(k).start()

    def clear(j, carry):
        kv[:, :, pl.ds(pl.multiple_of(j * rows, rows), rows), :] = jnp.zeros(
            (groups, 2, rows, HEAD_SIZE), jnp.bfloat16
        )
        return carry

    lax.fori_loop(s + 1, n_seq, clear, 0)

    forward(0)

    def step(c):
        @pl.when(c + 2 < groups)
        def _():
            own_out(c + 2)

        @pl.when(c + 1 < groups)
        def _():
            forward(c + 1)

        x_arrivals(c)
        compute(c)
        send_att(c)

        @pl.when(c > 0)
        def _():
            att_forward(c - 1)

    loop(step)
    att_forward(groups - 1)

    def drain(c):
        @pl.when(a < depth - 1)
        def _():
            z_copy(c, a).wait_send()

        @pl.when(b == 0)
        def _():
            x_copy(c, a).wait_send()

        for lag in range(1, depth):
            @pl.when(lag <= a)
            def _():
                x_copy(c, a - lag).wait_send()

                @pl.when(a < depth - 1)
                def _():
                    z_copy(c, a - lag).wait_send()

        att_local(c).wait()
        att_core(c).wait_send()
        att_arrived(c, mate)
        for k in range(1, far):
            att_far(c, k).wait_send()
            att_fwd(c, k).wait_send()
            att_arrived(c, 2 * lax.rem(y + k, far) + 1 - core)

    loop(drain)
    pltpu.make_async_copy(wt_ref, wts_hbm.at[n], w_local).wait()
    for k in range(1, n_node):
        w_copy(k).wait_send()
        origin = lax.rem(n + k, n_node)
        remote(wt_ref, wts_hbm.at[origin], w_send.at[k], w_recv.at[origin], mate, s).wait_recv()


def attend(n_node, n_seq, q, wt, k, v):
    rows = q.shape[0]
    groups, far = KEY_VALUE_HEADS, n_node // 2
    dma = pltpu.SemaphoreType.DMA
    return pl.pallas_call(
        functools.partial(attend_kernel, n_node, n_seq, rows),
        out_shape=(
            jax.ShapeDtypeStruct((n_node,) + q.shape, jnp.bfloat16),
            jax.ShapeDtypeStruct((n_node,) + wt.shape, jnp.float32),
        ),
        in_specs=[
            pl.BlockSpec(memory_space=pltpu.VMEM),
            pl.BlockSpec(memory_space=pltpu.VMEM),
            pl.BlockSpec(memory_space=pl.ANY),
            pl.BlockSpec(memory_space=pl.ANY),
        ],
        out_specs=(pl.BlockSpec(memory_space=pl.ANY), pl.BlockSpec(memory_space=pl.ANY)),
        scratch_shapes=[
            pltpu.VMEM((groups, 2, n_seq * rows, HEAD_SIZE), jnp.bfloat16),
            pltpu.VMEM(q.shape, jnp.bfloat16),
            dma((groups, 2)),
            dma((groups, n_seq)),
            dma((groups, n_seq // 2)),
            dma((groups, n_seq // 2)),
            dma((groups,)),
            dma((groups, n_node)),
            dma((groups,)),
            dma((groups, far)),
            dma((groups, far)),
            dma,
            dma((n_node,)),
            dma((n_node,)),
        ],
        compiler_params=pltpu.CompilerParams(
            collective_id=0, has_side_effects=True, vmem_limit_bytes=48 * 1024 * 1024
        ),
    )(q, wt, k, v)


def pick_kernel(cap, att_ref, wt_ref, out_ref):
    rows, width = att_ref.shape[1:]
    first = EXP_NODE * lax.axis_index("node")
    earlier = lax.broadcasted_iota(jnp.int32, (rows, rows), 0) < lax.broadcasted_iota(
        jnp.int32, (rows, rows), 1
    )
    earlier = earlier.astype(jnp.float32).astype(jnp.bfloat16)
    slots = lax.broadcasted_iota(jnp.int32, (cap, rows), 0).astype(jnp.float32)
    for e in range(EXP_NODE):
        weight = jnp.broadcast_to(wt_ref[0, pl.ds(first + e, 1), :], (8, rows))
        member = jnp.where(weight > 0, jnp.float32(1.0), jnp.float32(0.0))
        rank = jnp.dot(member.astype(jnp.bfloat16), earlier, preferred_element_type=jnp.float32)
        gate = jnp.broadcast_to(weight[:1], (cap, rows))
        place = jnp.broadcast_to(rank[:1], (cap, rows))
        table = jnp.where((gate > 0) & (place == slots), gate, 0.0).astype(jnp.bfloat16)
        for at in range(0, width, 1024):
            out_ref[e, 0, 0, :, at : at + 1024] = jnp.dot(
                table, att_ref[0, :, at : at + 1024], preferred_element_type=jnp.float32
            ).astype(jnp.bfloat16)


def pick(cap, att, wts):
    n_node, rows, width = att.shape
    return pl.pallas_call(
        functools.partial(pick_kernel, cap),
        grid=(n_node,),
        out_shape=jax.ShapeDtypeStruct((EXP_NODE, 1, n_node, cap, width), jnp.bfloat16),
        in_specs=[
            pl.BlockSpec((1, rows, width), lambda i: (i, 0, 0)),
            pl.BlockSpec((1,) + wts.shape[1:], lambda i: (i, 0, 0)),
        ],
        out_specs=pl.BlockSpec((EXP_NODE, 1, 1, cap, width), lambda i: (0, 0, i, 0, 0)),
        compiler_params=pltpu.CompilerParams(vmem_limit_bytes=32 * 1024 * 1024),
    )(att, wts)


def per_device(n_node, n_seq, queries, keys, values, routes, gates):
    experts = EXP_NODE * n_node
    cap = queries.shape[0] * TOP * 3 // (2 * experts)
    match = routes[None, :, :] == jnp.arange(experts, dtype=jnp.int32)[:, None, None]
    wt = jnp.sum(jnp.where(match, gates.astype(jnp.float32)[None], jnp.float32(0.0)), axis=2)
    att, wts = attend(n_node, n_seq, queries, wt, keys, values)
    return pick(cap, att, wts)


def solution(mesh):
    spec = P(("node", "seq"), None)
    return jax.shard_map(
        functools.partial(per_device, mesh.shape["node"], mesh.shape["seq"]),
        mesh=mesh,
        in_specs=(spec,) * 5,
        out_specs=P("node", "seq", None, None, None),
        check_vma=False,
    )
```

```python
import functools

import jax
import jax.numpy as jnp
from jax import lax
from jax.experimental import pallas as pl
from jax.experimental.pallas import tpu as pltpu
from jax.sharding import PartitionSpec as P

QUERY_HEADS = 32
KEY_VALUE_HEADS = 8
HEAD_SIZE = 128
TOP = 4
EXP_NODE = 2
MEMBERS = QUERY_HEADS // KEY_VALUE_HEADS
GROUP_COLS = MEMBERS * HEAD_SIZE
LOG2E = 1.4426950408889634
MESH = pl.DeviceIdType.MESH


def attend_kernel(
    n_node, n_seq, rows,
    wt_ref, q_hbm, k_hbm, v_hbm, all_hbm, wts_hbm,
    kv, qs, att, kv_local, kv_send, kv_recv, q_local, q_send, q_recv, z_send, z_recv,
    x_send, x_recv, a_local, a_recv, a_core, a_far, a_fwd, w_local, w_recv, w_send,
):
    n = lax.axis_index("node")
    s = lax.axis_index("seq")
    a, b = s // 2, lax.rem(s, 2)
    depth = n_seq // 2
    far = n_node // 2
    y, core = n // 2, lax.rem(n, 2)
    mate = 2 * y + 1 - core
    beside = 2 * a + 1 - b
    steps = KEY_VALUE_HEADS // 2

    def remote(src, dst, send, recv, node, seq):
        return pltpu.make_async_remote_copy(
            src_ref=src, dst_ref=dst, send_sem=send, recv_sem=recv,
            device_id=(node, seq), device_id_type=MESH,
        )

    def span_of(index, size):
        return pl.ds(pl.multiple_of(index * size, size), size)

    def kv_source(half, c, which):
        return (k_hbm, v_hbm)[which].at[:, span_of(half * steps + c, HEAD_SIZE)]

    def kv_rows(c, which, j):
        return kv.at[c, which, span_of(j, rows), :]

    def kv_keep(c, which):
        return pltpu.make_async_copy(
            kv_source(b, c, which), kv_rows(c, which, s), kv_local.at[c, which]
        )

    def kv_give(c, which):
        return remote(
            kv_source(1 - b, c, which), kv_rows(c, which, s),
            kv_send.at[c, which], kv_recv.at[c, which], n, beside,
        )

    def kv_taken(c, which):
        ref = kv_rows(c, which, beside)
        return remote(ref, ref, kv_send.at[c, which], kv_recv.at[c, which], n, beside)

    def q_source(half, c):
        return q_hbm.at[:, span_of(half * steps + c, GROUP_COLS)]

    def q_keep(c):
        return pltpu.make_async_copy(q_source(b, c), qs.at[c, b], q_local.at[c])

    def q_give(c):
        return remote(
            q_source(1 - b, c), qs.at[c, b], q_send.at[c], q_recv.at[c], n, beside
        )

    def q_taken(c):
        ref = qs.at[c, 1 - b]
        return remote(ref, ref, q_send.at[c], q_recv.at[c], n, beside)

    def z_copy(c, line):
        ref = kv.at[c, :, span_of(line, 2 * rows), :]
        return remote(ref, ref, z_send.at[c, line], z_recv.at[c, line], n, s + 2)

    def z_arrived(c, line):
        ref = kv.at[c, :, span_of(line, 2 * rows), :]
        remote(ref, ref, z_send.at[c, line], z_recv.at[c, line], n, beside).wait_recv()

    def loop(body):
        def step(c, carry):
            body(c)
            return carry
        lax.fori_loop(0, steps, step, 0)

    def load(c):
        kv_keep(c, 0).start()
        kv_keep(c, 1).start()
        q_keep(c).start()

    loop(load)

    barrier = pltpu.get_barrier_semaphore()

    def greet(node, seq):
        pl.semaphore_signal(barrier, inc=1, device_id=(node, seq), device_id_type=MESH)

    greet(n, beside)
    for k in range(1, n_node):
        greet(lax.rem(n + k, n_node), s)

    @pl.when(a > 0)
    def _():
        greet(n, s - 2)

    @pl.when(a < depth - 1)
    def _():
        greet(n, s + 2)

    edges = (a > 0).astype(jnp.int32) + (a < depth - 1).astype(jnp.int32)
    pl.semaphore_wait(barrier, n_node + edges)

    def give_kv(c):
        kv_give(c, 0).start()
        kv_give(c, 1).start()

    loop(give_kv)
    loop(lambda c: q_give(c).start())

    def pair_out(c):
        for which in range(2):
            kv_keep(c, which).wait()
            kv_taken(c, which).wait_recv()

        @pl.when(a < depth - 1)
        def _():
            z_copy(c, a).start()

    def forward(c, send):
        for lag in range(1, depth):
            @pl.when(lag <= a)
            def _():
                z_arrived(c, a - lag)
                if send:
                    z_copy(c, a - lag).start()

    def landing(half, c, node):
        return all_hbm.at[node, :, span_of(half * steps + c, GROUP_COLS)]

    def x_give(c):
        return remote(att.at[c, 1 - b], landing(b, c, n), x_send.at[c], x_recv.at[c], n, beside)

    def x_taken(c):
        ref = landing(1 - b, c, n)
        return remote(ref, ref, x_send.at[c], x_recv.at[c], n, beside)

    def att_local(c):
        return pltpu.make_async_copy(att.at[c, b], landing(b, c, n), a_local.at[c])

    def att_from(own, half, c):
        return att.at[c, b] if own else landing(half, c, n)

    def att_core(own, half, c):
        return remote(
            att_from(own, half, c), landing(half, c, n),
            a_core.at[half, c], a_recv.at[half, c, n], mate, s,
        )

    def att_far(own, half, c, k):
        other = 2 * lax.rem(y + k, far) + core
        return remote(
            att_from(own, half, c), landing(half, c, n),
            a_far.at[half, c, k], a_recv.at[half, c, n], other, s,
        )

    def att_fwd(half, c, k):
        origin = 2 * lax.rem(y + k, far) + core
        ref = landing(half, c, origin)
        return remote(ref, ref, a_fwd.at[half, c, k], a_recv.at[half, c, origin], mate, s)

    def att_arrived(half, c, node):
        ref = landing(half, c, node)
        remote(ref, ref, a_core.at[half, c], a_recv.at[half, c, node], mate, s).wait_recv()

    def att_forward(half, c):
        for k in range(1, far):
            att_arrived(half, c, 2 * lax.rem(y + k, far) + core)
            att_fwd(half, c, k).start()

    def spread(own, half, c):
        for k in range(1, far):
            att_far(own, half, c, k).start()
        att_core(own, half, c).start()

    def relay(c):
        x_taken(c).wait_recv()
        spread(False, 1 - b, c)

    span = n_seq * rows
    key_pos = lax.broadcasted_iota(jnp.int32, (rows, span), 1)
    row_at = lax.broadcasted_iota(jnp.int32, (rows, span), 0)

    def compute(c, p):
        allowed = key_pos - row_at <= (2 * a + p) * rows
        allowed = jnp.concatenate([allowed] * MEMBERS, axis=0)
        q_part = qs[c, p]
        stacked = jnp.concatenate(
            [q_part[:, h * HEAD_SIZE : (h + 1) * HEAD_SIZE] for h in range(MEMBERS)], axis=0
        )
        scores = lax.dot_general(
            stacked, kv[c, 0], (((1,), (1,)), ((), ())), preferred_element_type=jnp.float32
        )
        scores = jnp.where(allowed, scores, jnp.float32(-1e30))
        top = jnp.max(scores, axis=1, keepdims=True)
        raised = jnp.exp2((scores - top) * jnp.float32(HEAD_SIZE ** -0.5 * LOG2E))
        total = jnp.sum(raised, axis=1, keepdims=True)
        shares = (raised * (1.0 / total)).astype(jnp.bfloat16)
        result = jnp.dot(shares, kv[c, 1], preferred_element_type=jnp.float32).astype(jnp.bfloat16)
        for h in range(MEMBERS):
            att[c, p, :, h * HEAD_SIZE : (h + 1) * HEAD_SIZE] = result[h * rows : (h + 1) * rows]

    def w_copy(k):
        other = lax.rem(n + k, n_node)
        return remote(wt_ref, wts_hbm.at[n], w_send.at[k], w_recv.at[n], other, s)

    def clear(j, carry):
        kv[:, :, span_of(j, rows), :] = jnp.zeros((steps, 2, rows, HEAD_SIZE), jnp.bfloat16)
        return carry

    lax.fori_loop(2 * a + 2, n_seq, clear, 0)
    pair_out(0)
    pair_out(1)

    pltpu.make_async_copy(wt_ref, wts_hbm.at[n], w_local).start()
    for k in range(1, n_node):
        w_copy(k).start()

    @pl.when(a < depth - 1)
    def _():
        forward(0, True)

    def step(c):
        @pl.when(c + 2 < steps)
        def _():
            pair_out(c + 2)

        @pl.when((a < depth - 1) & (c + 1 < steps))
        def _():
            forward(c + 1, True)

        @pl.when(a == depth - 1)
        def _():
            forward(c, False)

        q_taken(c).wait_recv()
        compute(c, 1 - b)
        x_give(c).start()

        @pl.when(c > 0)
        def _():
            relay(c - 1)

        q_keep(c).wait()
        compute(c, b)
        att_local(c).start()
        spread(True, b, c)

        @pl.when(c > 0)
        def _():
            att_forward(b, c - 1)
            att_forward(1 - b, c - 1)

    loop(step)
    relay(steps - 1)
    att_forward(b, steps - 1)
    att_forward(1 - b, steps - 1)

    def drain(c):
        for which in range(2):
            kv_give(c, which).wait_send()
        q_give(c).wait_send()
        x_give(c).wait_send()

        @pl.when(a < depth - 1)
        def _():
            for lag in range(depth):
                @pl.when(lag <= a)
                def _():
                    z_copy(c, a - lag).wait_send()

        att_local(c).wait()
        for own in (True, False):
            half = b if own else 1 - b
            att_core(own, half, c).wait_send()
            att_arrived(half, c, mate)
            for k in range(1, far):
                att_far(own, half, c, k).wait_send()
                att_fwd(half, c, k).wait_send()
                att_arrived(half, c, 2 * lax.rem(y + k, far) + 1 - core)

    loop(drain)
    pltpu.make_async_copy(wt_ref, wts_hbm.at[n], w_local).wait()
    for k in range(1, n_node):
        w_copy(k).wait_send()
        origin = lax.rem(n + k, n_node)
        remote(wt_ref, wts_hbm.at[origin], w_send.at[k], w_recv.at[origin], mate, s).wait_recv()


def attend(n_node, n_seq, q, wt, k, v):
    rows = q.shape[0]
    steps, far, depth = KEY_VALUE_HEADS // 2, n_node // 2, n_seq // 2
    dma = pltpu.SemaphoreType.DMA
    hbm = pl.BlockSpec(memory_space=pl.ANY)
    return pl.pallas_call(
        functools.partial(attend_kernel, n_node, n_seq, rows),
        out_shape=(
            jax.ShapeDtypeStruct((n_node,) + q.shape, jnp.bfloat16),
            jax.ShapeDtypeStruct((n_node,) + wt.shape, jnp.float32),
        ),
        in_specs=[pl.BlockSpec(memory_space=pltpu.VMEM), hbm, hbm, hbm],
        out_specs=(hbm, hbm),
        scratch_shapes=[
            pltpu.VMEM((steps, 2, n_seq * rows, HEAD_SIZE), jnp.bfloat16),
            pltpu.VMEM((steps, 2, rows, GROUP_COLS), jnp.bfloat16),
            pltpu.VMEM((steps, 2, rows, GROUP_COLS), jnp.bfloat16),
            dma((steps, 2)), dma((steps, 2)), dma((steps, 2)),
            dma((steps,)), dma((steps,)), dma((steps,)),
            dma((steps, depth)), dma((steps, depth)),
            dma((steps,)), dma((steps,)),
            dma((steps,)),
            dma((2, steps, n_node)),
            dma((2, steps)),
            dma((2, steps, far)),
            dma((2, steps, far)),
            dma,
            dma((n_node,)),
            dma((n_node,)),
        ],
        compiler_params=pltpu.CompilerParams(
            collective_id=0, has_side_effects=True, vmem_limit_bytes=60 * 1024 * 1024
        ),
    )(wt, q, k, v)


def pick_kernel(cap, att_ref, wt_ref, out_ref):
    rows, width = att_ref.shape[1:]
    first = EXP_NODE * lax.axis_index("node")
    earlier = lax.broadcasted_iota(jnp.int32, (rows, rows), 0) < lax.broadcasted_iota(
        jnp.int32, (rows, rows), 1
    )
    earlier = earlier.astype(jnp.float32).astype(jnp.bfloat16)
    slots = lax.broadcasted_iota(jnp.int32, (cap, rows), 0).astype(jnp.float32)
    for e in range(EXP_NODE):
        weight = jnp.broadcast_to(wt_ref[0, pl.ds(first + e, 1), :], (8, rows))
        member = jnp.where(weight > 0, jnp.float32(1.0), jnp.float32(0.0))
        rank = jnp.dot(member.astype(jnp.bfloat16), earlier, preferred_element_type=jnp.float32)
        gate = jnp.broadcast_to(weight[:1], (cap, rows))
        place = jnp.broadcast_to(rank[:1], (cap, rows))
        table = jnp.where((gate > 0) & (place == slots), gate, 0.0).astype(jnp.bfloat16)
        for at in range(0, width, 1024):
            out_ref[e, 0, 0, :, at : at + 1024] = jnp.dot(
                table, att_ref[0, :, at : at + 1024], preferred_element_type=jnp.float32
            ).astype(jnp.bfloat16)


def pick(cap, att, wts):
    n_node, rows, width = att.shape
    return pl.pallas_call(
        functools.partial(pick_kernel, cap),
        grid=(n_node,),
        out_shape=jax.ShapeDtypeStruct((EXP_NODE, 1, n_node, cap, width), jnp.bfloat16),
        in_specs=[
            pl.BlockSpec((1, rows, width), lambda i: (i, 0, 0)),
            pl.BlockSpec((1,) + wts.shape[1:], lambda i: (i, 0, 0)),
        ],
        out_specs=pl.BlockSpec((EXP_NODE, 1, 1, cap, width), lambda i: (0, 0, i, 0, 0)),
        compiler_params=pltpu.CompilerParams(vmem_limit_bytes=60 * 1024 * 1024),
    )(att, wts)


def per_device(n_node, n_seq, queries, keys, values, routes, gates):
    experts = EXP_NODE * n_node
    cap = queries.shape[0] * TOP * 3 // (2 * experts)
    match = routes[None, :, :] == jnp.arange(experts, dtype=jnp.int32)[:, None, None]
    wt = jnp.sum(jnp.where(match, gates.astype(jnp.float32)[None], jnp.float32(0.0)), axis=2)
    att, wts = attend(n_node, n_seq, queries, wt, keys, values)
    return pick(cap, att, wts)


def solution(mesh):
    spec = P(("node", "seq"), None)
    return jax.shard_map(
        functools.partial(per_device, mesh.shape["node"], mesh.shape["seq"]),
        mesh=mesh,
        in_specs=(spec,) * 5,
        out_specs=P("node", "seq", None, None, None),
        check_vma=False,
    )
```

```python
import functools

import jax
import jax.numpy as jnp
from jax import lax
from jax.experimental import pallas as pl
from jax.experimental.pallas import tpu as pltpu
from jax.sharding import PartitionSpec as P

QUERY_HEADS = 32
KEY_VALUE_HEADS = 8
HEAD_SIZE = 128
TOP = 4
EXP_NODE = 2
MEMBERS = QUERY_HEADS // KEY_VALUE_HEADS
GROUP_COLS = MEMBERS * HEAD_SIZE
LOG2E = 1.4426950408889634
MESH = pl.DeviceIdType.MESH


def attend_kernel(
    n_node, n_seq, rows,
    wt_ref, q_hbm, k_hbm, v_hbm, all_hbm, wts_hbm,
    kv, qs, att, kv_local, kv_send, kv_recv, q_local, q_send, q_recv, z_send, z_recv,
    x_send, x_recv, a_local, a_recv, a_core, a_far, a_fwd, w_local, w_recv, w_send,
):
    n = lax.axis_index("node")
    s = lax.axis_index("seq")
    a, b = s // 2, lax.rem(s, 2)
    depth = n_seq // 2
    far = n_node // 2
    y, core = n // 2, lax.rem(n, 2)
    mate = 2 * y + 1 - core
    beside = 2 * a + 1 - b
    steps = KEY_VALUE_HEADS // 2

    def remote(src, dst, send, recv, node, seq):
        return pltpu.make_async_remote_copy(
            src_ref=src, dst_ref=dst, send_sem=send, recv_sem=recv,
            device_id=(node, seq), device_id_type=MESH,
        )

    def span_of(index, size):
        return pl.ds(pl.multiple_of(index * size, size), size)

    def kv_source(half, c, which):
        return (k_hbm, v_hbm)[which].at[:, span_of(half * steps + c, HEAD_SIZE)]

    def kv_rows(c, which, j):
        return kv.at[c, which, span_of(j, rows), :]

    def kv_keep(c, which):
        return pltpu.make_async_copy(
            kv_source(b, c, which), kv_rows(c, which, s), kv_local.at[c, which]
        )

    def kv_give(c, which):
        return remote(
            kv_source(1 - b, c, which), kv_rows(c, which, s),
            kv_send.at[c, which], kv_recv.at[c, which], n, beside,
        )

    def kv_taken(c, which):
        ref = kv_rows(c, which, beside)
        return remote(ref, ref, kv_send.at[c, which], kv_recv.at[c, which], n, beside)

    def q_source(half, c):
        return q_hbm.at[:, span_of(half * steps + c, GROUP_COLS)]

    def q_keep(c):
        return pltpu.make_async_copy(q_source(b, c), qs.at[c, b], q_local.at[c])

    def q_give(c):
        return remote(
            q_source(1 - b, c), qs.at[c, b], q_send.at[c], q_recv.at[c], n, beside
        )

    def q_taken(c):
        ref = qs.at[c, 1 - b]
        return remote(ref, ref, q_send.at[c], q_recv.at[c], n, beside)

    def z_copy(c, line):
        ref = kv.at[c, :, span_of(line, 2 * rows), :]
        return remote(ref, ref, z_send.at[c, line], z_recv.at[c, line], n, s + 2)

    def z_part(c, j):
        ref = kv.at[c, :, span_of(j, rows), :]
        return remote(ref, ref, z_send.at[c, a], z_recv.at[c, a], n, s + 2)

    def z_arrived(c, line):
        ref = kv.at[c, :, span_of(line, 2 * rows), :]
        remote(ref, ref, z_send.at[c, line], z_recv.at[c, line], n, beside).wait_recv()

    def loop(body):
        def step(c, carry):
            body(c)
            return carry
        lax.fori_loop(0, steps, step, 0)

    def load(c):
        kv_keep(c, 0).start()
        kv_keep(c, 1).start()
        q_keep(c).start()

    loop(load)

    barrier = pltpu.get_barrier_semaphore()

    def greet(node, seq):
        pl.semaphore_signal(barrier, inc=1, device_id=(node, seq), device_id_type=MESH)

    greet(n, beside)
    for k in range(1, n_node):
        greet(lax.rem(n + k, n_node), s)

    @pl.when(a > 0)
    def _():
        greet(n, s - 2)

    @pl.when(a < depth - 1)
    def _():
        greet(n, s + 2)

    edges = (a > 0).astype(jnp.int32) + (a < depth - 1).astype(jnp.int32)
    pl.semaphore_wait(barrier, n_node + edges)

    def give_kv(c):
        kv_give(c, 0).start()
        kv_give(c, 1).start()

    loop(give_kv)

    def own_out(c):
        for which in range(2):
            kv_keep(c, which).wait()

        @pl.when(a < depth - 1)
        def _():
            z_part(c, s).start()

    loop(own_out)
    loop(lambda c: q_give(c).start())

    def pair_out(c):
        for which in range(2):
            kv_taken(c, which).wait_recv()

        @pl.when(a < depth - 1)
        def _():
            z_part(c, beside).start()

    def forward(c, send):
        for lag in range(1, depth):
            @pl.when(lag <= a)
            def _():
                z_arrived(c, a - lag)
                if send:
                    z_copy(c, a - lag).start()

    def landing(half, c, node):
        return all_hbm.at[node, :, span_of(half * steps + c, GROUP_COLS)]

    def x_give(c):
        return remote(att.at[c, 1 - b], landing(b, c, n), x_send.at[c], x_recv.at[c], n, beside)

    def x_taken(c):
        ref = landing(1 - b, c, n)
        return remote(ref, ref, x_send.at[c], x_recv.at[c], n, beside)

    def att_local(c):
        return pltpu.make_async_copy(att.at[c, b], landing(b, c, n), a_local.at[c])

    def att_from(own, half, c):
        return att.at[c, b] if own else landing(half, c, n)

    def att_core(own, half, c):
        return remote(
            att_from(own, half, c), landing(half, c, n),
            a_core.at[half, c], a_recv.at[half, c, n], mate, s,
        )

    def att_far(own, half, c, k):
        other = 2 * lax.rem(y + k, far) + core
        return remote(
            att_from(own, half, c), landing(half, c, n),
            a_far.at[half, c, k], a_recv.at[half, c, n], other, s,
        )

    def att_fwd(half, c, k):
        origin = 2 * lax.rem(y + k, far) + core
        ref = landing(half, c, origin)
        return remote(ref, ref, a_fwd.at[half, c, k], a_recv.at[half, c, origin], mate, s)

    def att_arrived(half, c, node):
        ref = landing(half, c, node)
        remote(ref, ref, a_core.at[half, c], a_recv.at[half, c, node], mate, s).wait_recv()

    def att_forward(half, c):
        for k in range(1, far):
            att_arrived(half, c, 2 * lax.rem(y + k, far) + core)
            att_fwd(half, c, k).start()

    def spread(own, half, c):
        for k in range(1, far):
            att_far(own, half, c, k).start()
        att_core(own, half, c).start()

    def relay(c):
        x_taken(c).wait_recv()
        spread(False, 1 - b, c)

    span = n_seq * rows
    key_pos = lax.broadcasted_iota(jnp.int32, (rows, span), 1)
    row_at = lax.broadcasted_iota(jnp.int32, (rows, span), 0)

    def compute(c, p):
        allowed = key_pos - row_at <= (2 * a + p) * rows
        allowed = jnp.concatenate([allowed] * MEMBERS, axis=0)
        q_part = qs[c, p]
        stacked = jnp.concatenate(
            [q_part[:, h * HEAD_SIZE : (h + 1) * HEAD_SIZE] for h in range(MEMBERS)], axis=0
        )
        scores = lax.dot_general(
            stacked, kv[c, 0], (((1,), (1,)), ((), ())), preferred_element_type=jnp.float32
        )
        scores = jnp.where(allowed, scores, jnp.float32(-1e30))
        top = jnp.max(scores, axis=1, keepdims=True)
        raised = jnp.exp2((scores - top) * jnp.float32(HEAD_SIZE ** -0.5 * LOG2E))
        total = jnp.sum(raised, axis=1, keepdims=True)
        shares = (raised * (1.0 / total)).astype(jnp.bfloat16)
        result = jnp.dot(shares, kv[c, 1], preferred_element_type=jnp.float32).astype(jnp.bfloat16)
        for h in range(MEMBERS):
            att[c, p, :, h * HEAD_SIZE : (h + 1) * HEAD_SIZE] = result[h * rows : (h + 1) * rows]

    def w_copy(k):
        other = lax.rem(n + k, n_node)
        return remote(wt_ref, wts_hbm.at[n], w_send.at[k], w_recv.at[n], other, s)

    def clear(j, carry):
        kv[:, :, span_of(j, rows), :] = jnp.zeros((steps, 2, rows, HEAD_SIZE), jnp.bfloat16)
        return carry

    lax.fori_loop(2 * a + 2, n_seq, clear, 0)
    pair_out(0)
    pair_out(1)

    pltpu.make_async_copy(wt_ref, wts_hbm.at[n], w_local).start()
    for k in range(1, n_node):
        w_copy(k).start()

    @pl.when(a < depth - 1)
    def _():
        forward(0, True)

    def step(c):
        @pl.when(c + 2 < steps)
        def _():
            pair_out(c + 2)

        @pl.when((a < depth - 1) & (c + 1 < steps))
        def _():
            forward(c + 1, True)

        @pl.when(a == depth - 1)
        def _():
            forward(c, False)

        q_taken(c).wait_recv()
        compute(c, 1 - b)
        x_give(c).start()

        @pl.when(c > 0)
        def _():
            relay(c - 1)

        q_keep(c).wait()
        compute(c, b)
        att_local(c).start()
        spread(True, b, c)

        @pl.when(c > 0)
        def _():
            att_forward(b, c - 1)
            att_forward(1 - b, c - 1)

    loop(step)
    relay(steps - 1)
    att_forward(b, steps - 1)
    att_forward(1 - b, steps - 1)

    def drain(c):
        for which in range(2):
            kv_give(c, which).wait_send()
        q_give(c).wait_send()
        x_give(c).wait_send()

        @pl.when(a < depth - 1)
        def _():
            for lag in range(depth):
                @pl.when(lag <= a)
                def _():
                    z_copy(c, a - lag).wait_send()

        att_local(c).wait()
        for own in (True, False):
            half = b if own else 1 - b
            att_core(own, half, c).wait_send()
            att_arrived(half, c, mate)
            for k in range(1, far):
                att_far(own, half, c, k).wait_send()
                att_fwd(half, c, k).wait_send()
                att_arrived(half, c, 2 * lax.rem(y + k, far) + 1 - core)

    loop(drain)
    pltpu.make_async_copy(wt_ref, wts_hbm.at[n], w_local).wait()
    for k in range(1, n_node):
        w_copy(k).wait_send()
        origin = lax.rem(n + k, n_node)
        remote(wt_ref, wts_hbm.at[origin], w_send.at[k], w_recv.at[origin], mate, s).wait_recv()


def attend(n_node, n_seq, q, wt, k, v):
    rows = q.shape[0]
    steps, far, depth = KEY_VALUE_HEADS // 2, n_node // 2, n_seq // 2
    dma = pltpu.SemaphoreType.DMA
    hbm = pl.BlockSpec(memory_space=pl.ANY)
    return pl.pallas_call(
        functools.partial(attend_kernel, n_node, n_seq, rows),
        out_shape=(
            jax.ShapeDtypeStruct((n_node,) + q.shape, jnp.bfloat16),
            jax.ShapeDtypeStruct((n_node,) + wt.shape, jnp.float32),
        ),
        in_specs=[pl.BlockSpec(memory_space=pltpu.VMEM), hbm, hbm, hbm],
        out_specs=(hbm, hbm),
        scratch_shapes=[
            pltpu.VMEM((steps, 2, n_seq * rows, HEAD_SIZE), jnp.bfloat16),
            pltpu.VMEM((steps, 2, rows, GROUP_COLS), jnp.bfloat16),
            pltpu.VMEM((steps, 2, rows, GROUP_COLS), jnp.bfloat16),
            dma((steps, 2)), dma((steps, 2)), dma((steps, 2)),
            dma((steps,)), dma((steps,)), dma((steps,)),
            dma((steps, depth)), dma((steps, depth)),
            dma((steps,)), dma((steps,)),
            dma((steps,)),
            dma((2, steps, n_node)),
            dma((2, steps)),
            dma((2, steps, far)),
            dma((2, steps, far)),
            dma,
            dma((n_node,)),
            dma((n_node,)),
        ],
        compiler_params=pltpu.CompilerParams(
            collective_id=0, has_side_effects=True, vmem_limit_bytes=60 * 1024 * 1024
        ),
    )(wt, q, k, v)


def pick_kernel(cap, att_ref, wt_ref, out_ref):
    rows, width = att_ref.shape[1:]
    first = EXP_NODE * lax.axis_index("node")
    earlier = lax.broadcasted_iota(jnp.int32, (rows, rows), 0) < lax.broadcasted_iota(
        jnp.int32, (rows, rows), 1
    )
    earlier = earlier.astype(jnp.float32).astype(jnp.bfloat16)
    slots = lax.broadcasted_iota(jnp.int32, (cap, rows), 0).astype(jnp.float32)
    tables = []
    for e in range(EXP_NODE):
        weight = jnp.broadcast_to(wt_ref[0, pl.ds(first + e, 1), :], (8, rows))
        member = jnp.where(weight > 0, jnp.float32(1.0), jnp.float32(0.0))
        rank = jnp.dot(member.astype(jnp.bfloat16), earlier, preferred_element_type=jnp.float32)
        gate = jnp.broadcast_to(weight[:1], (cap, rows))
        place = jnp.broadcast_to(rank[:1], (cap, rows))
        tables.append(jnp.where((gate > 0) & (place == slots), gate, 0.0).astype(jnp.bfloat16))
    table = jnp.concatenate(tables, axis=0)
    for at in range(0, width, 512):
        rows_out = jnp.dot(
            table, att_ref[0, :, at : at + 512], preferred_element_type=jnp.float32
        ).astype(jnp.bfloat16)
        for e in range(EXP_NODE):
            out_ref[e, 0, 0, :, at : at + 512] = rows_out[e * cap : (e + 1) * cap]


def pick(cap, att, wts):
    n_node, rows, width = att.shape
    return pl.pallas_call(
        functools.partial(pick_kernel, cap),
        grid=(n_node,),
        out_shape=jax.ShapeDtypeStruct((EXP_NODE, 1, n_node, cap, width), jnp.bfloat16),
        in_specs=[
            pl.BlockSpec((1, rows, width), lambda i: (i, 0, 0)),
            pl.BlockSpec((1,) + wts.shape[1:], lambda i: (i, 0, 0)),
        ],
        out_specs=pl.BlockSpec((EXP_NODE, 1, 1, cap, width), lambda i: (0, 0, i, 0, 0)),
        compiler_params=pltpu.CompilerParams(vmem_limit_bytes=60 * 1024 * 1024),
    )(att, wts)


def per_device(n_node, n_seq, queries, keys, values, routes, gates):
    experts = EXP_NODE * n_node
    cap = queries.shape[0] * TOP * 3 // (2 * experts)
    match = routes[None, :, :] == jnp.arange(experts, dtype=jnp.int32)[:, None, None]
    wt = jnp.sum(jnp.where(match, gates.astype(jnp.float32)[None], jnp.float32(0.0)), axis=2)
    att, wts = attend(n_node, n_seq, queries, wt, keys, values)
    return pick(cap, att, wts)


def solution(mesh):
    spec = P(("node", "seq"), None)
    return jax.shard_map(
        functools.partial(per_device, mesh.shape["node"], mesh.shape["seq"]),
        mesh=mesh,
        in_specs=(spec,) * 5,
        out_specs=P("node", "seq", None, None, None),
        check_vma=False,
    )
```

```python
import functools

import jax
import jax.numpy as jnp
from jax import lax
from jax.experimental import pallas as pl
from jax.experimental.pallas import tpu as pltpu
from jax.sharding import PartitionSpec as P

QUERY_HEADS = 32
KEY_VALUE_HEADS = 8
HEAD_SIZE = 128
TOP = 4
EXP_NODE = 2
MEMBERS = QUERY_HEADS // KEY_VALUE_HEADS
GROUP_COLS = MEMBERS * HEAD_SIZE
LOG2E = 1.4426950408889634
MESH = pl.DeviceIdType.MESH


def attend_kernel(
    n_node, n_seq, rows,
    wt_ref, q_hbm, k_hbm, v_hbm, all_hbm, wts_hbm,
    kv, qs, att, kv_local, kv_send, kv_recv, q_local, q_send, q_recv, z_send, z_recv,
    x_send, x_recv, a_local, a_recv, a_core, a_far, a_fwd, w_local, w_recv, w_send,
):
    n = lax.axis_index("node")
    s = lax.axis_index("seq")
    a, b = s // 2, lax.rem(s, 2)
    depth = n_seq // 2
    far = n_node // 2
    y, core = n // 2, lax.rem(n, 2)
    mate = 2 * y + 1 - core
    beside = 2 * a + 1 - b
    steps = KEY_VALUE_HEADS // 2

    def remote(src, dst, send, recv, node, seq):
        return pltpu.make_async_remote_copy(
            src_ref=src, dst_ref=dst, send_sem=send, recv_sem=recv,
            device_id=(node, seq), device_id_type=MESH,
        )

    def span_of(index, size):
        return pl.ds(pl.multiple_of(index * size, size), size)

    def kv_source(half, c, which):
        return (k_hbm, v_hbm)[which].at[:, span_of(half * steps + c, HEAD_SIZE)]

    def kv_rows(c, which, j):
        return kv.at[c, which, span_of(j, rows), :]

    def kv_keep(c, which):
        return pltpu.make_async_copy(
            kv_source(b, c, which), kv_rows(c, which, s), kv_local.at[c, which]
        )

    def kv_give(c, which):
        return remote(
            kv_source(1 - b, c, which), kv_rows(c, which, s),
            kv_send.at[c, which], kv_recv.at[c, which], n, beside,
        )

    def kv_taken(c, which):
        ref = kv_rows(c, which, beside)
        return remote(ref, ref, kv_send.at[c, which], kv_recv.at[c, which], n, beside)

    def q_source(half, c):
        return q_hbm.at[:, span_of(half * steps + c, GROUP_COLS)]

    def q_keep(c):
        return pltpu.make_async_copy(q_source(b, c), qs.at[c, b], q_local.at[c])

    def q_give(c):
        return remote(
            q_source(1 - b, c), qs.at[c, b], q_send.at[c], q_recv.at[c], n, beside
        )

    def q_taken(c):
        ref = qs.at[c, 1 - b]
        return remote(ref, ref, q_send.at[c], q_recv.at[c], n, beside)

    def z_copy(c, line):
        ref = kv.at[c, :, span_of(line, 2 * rows), :]
        return remote(ref, ref, z_send.at[c, line], z_recv.at[c, line], n, s + 2)

    def z_part(c, j):
        ref = kv.at[c, :, span_of(j, rows), :]
        return remote(ref, ref, z_send.at[c, a], z_recv.at[c, a], n, s + 2)

    def z_arrived(c, line):
        ref = kv.at[c, :, span_of(line, 2 * rows), :]
        remote(ref, ref, z_send.at[c, line], z_recv.at[c, line], n, beside).wait_recv()

    def loop(body):
        def step(c, carry):
            body(c)
            return carry
        lax.fori_loop(0, steps, step, 0)

    def load(c):
        kv_keep(c, 0).start()
        kv_keep(c, 1).start()
        q_keep(c).start()

    loop(load)

    barrier = pltpu.get_barrier_semaphore()

    def greet(node, seq):
        pl.semaphore_signal(barrier, inc=1, device_id=(node, seq), device_id_type=MESH)

    greet(n, beside)
    for k in range(1, n_node):
        greet(lax.rem(n + k, n_node), s)

    @pl.when(a > 0)
    def _():
        greet(n, s - 2)

    @pl.when(a < depth - 1)
    def _():
        greet(n, s + 2)

    edges = (a > 0).astype(jnp.int32) + (a < depth - 1).astype(jnp.int32)
    pl.semaphore_wait(barrier, n_node + edges)

    def give_kv(c):
        kv_give(c, 0).start()
        kv_give(c, 1).start()

    loop(give_kv)

    def own_out(c):
        for which in range(2):
            kv_keep(c, which).wait()

        @pl.when(a < depth - 1)
        def _():
            z_part(c, s).start()

    loop(own_out)
    q_give(0).start()

    def pair_out(c):
        for which in range(2):
            kv_taken(c, which).wait_recv()

        @pl.when(a < depth - 1)
        def _():
            z_part(c, beside).start()

    def forward(c, send):
        for lag in range(1, depth):
            @pl.when(lag <= a)
            def _():
                z_arrived(c, a - lag)
                if send:
                    z_copy(c, a - lag).start()

    def landing(half, c, node):
        return all_hbm.at[node, :, span_of(half * steps + c, GROUP_COLS)]

    def x_give(c):
        return remote(att.at[c, 1 - b], landing(b, c, n), x_send.at[c], x_recv.at[c], n, beside)

    def x_taken(c):
        ref = landing(1 - b, c, n)
        return remote(ref, ref, x_send.at[c], x_recv.at[c], n, beside)

    def att_local(c):
        return pltpu.make_async_copy(att.at[c, b], landing(b, c, n), a_local.at[c])

    def att_from(own, half, c):
        return att.at[c, b] if own else landing(half, c, n)

    def att_core(own, half, c):
        return remote(
            att_from(own, half, c), landing(half, c, n),
            a_core.at[half, c], a_recv.at[half, c, n], mate, s,
        )

    def att_far(own, half, c, k):
        other = 2 * lax.rem(y + k, far) + core
        return remote(
            att_from(own, half, c), landing(half, c, n),
            a_far.at[half, c, k], a_recv.at[half, c, n], other, s,
        )

    def att_fwd(half, c, k):
        origin = 2 * lax.rem(y + k, far) + core
        ref = landing(half, c, origin)
        return remote(ref, ref, a_fwd.at[half, c, k], a_recv.at[half, c, origin], mate, s)

    def att_arrived(half, c, node):
        ref = landing(half, c, node)
        remote(ref, ref, a_core.at[half, c], a_recv.at[half, c, node], mate, s).wait_recv()

    def att_forward(half, c):
        for k in range(1, far):
            att_arrived(half, c, 2 * lax.rem(y + k, far) + core)
            att_fwd(half, c, k).start()

    def spread(own, half, c):
        for k in range(1, far):
            att_far(own, half, c, k).start()
        att_core(own, half, c).start()

    def relay(c):
        x_taken(c).wait_recv()
        spread(False, 1 - b, c)

    span = n_seq * rows
    key_pos = lax.broadcasted_iota(jnp.int32, (rows, span), 1)
    row_at = lax.broadcasted_iota(jnp.int32, (rows, span), 0)

    def compute(c, p):
        allowed = key_pos - row_at <= (2 * a + p) * rows
        allowed = jnp.concatenate([allowed] * MEMBERS, axis=0)
        q_part = qs[c, p]
        stacked = jnp.concatenate(
            [q_part[:, h * HEAD_SIZE : (h + 1) * HEAD_SIZE] for h in range(MEMBERS)], axis=0
        )
        scores = lax.dot_general(
            stacked, kv[c, 0], (((1,), (1,)), ((), ())), preferred_element_type=jnp.float32
        )
        scores = jnp.where(allowed, scores, jnp.float32(-1e30))
        top = jnp.max(scores, axis=1, keepdims=True)
        raised = jnp.exp2((scores - top) * jnp.float32(HEAD_SIZE ** -0.5 * LOG2E))
        total = jnp.sum(raised, axis=1, keepdims=True)
        shares = (raised * (1.0 / total)).astype(jnp.bfloat16)
        result = jnp.dot(shares, kv[c, 1], preferred_element_type=jnp.float32).astype(jnp.bfloat16)
        for h in range(MEMBERS):
            att[c, p, :, h * HEAD_SIZE : (h + 1) * HEAD_SIZE] = result[h * rows : (h + 1) * rows]

    def w_copy(k):
        other = lax.rem(n + k, n_node)
        return remote(wt_ref, wts_hbm.at[n], w_send.at[k], w_recv.at[n], other, s)

    def clear(j, carry):
        kv[:, :, span_of(j, rows), :] = jnp.zeros((steps, 2, rows, HEAD_SIZE), jnp.bfloat16)
        return carry

    lax.fori_loop(2 * a + 2, n_seq, clear, 0)
    pair_out(0)
    pair_out(1)

    pltpu.make_async_copy(wt_ref, wts_hbm.at[n], w_local).start()
    for k in range(1, n_node):
        w_copy(k).start()

    @pl.when(a < depth - 1)
    def _():
        forward(0, True)

    def step(c):
        @pl.when(c + 2 < steps)
        def _():
            pair_out(c + 2)

        @pl.when((a < depth - 1) & (c + 1 < steps))
        def _():
            forward(c + 1, True)

        @pl.when(a == depth - 1)
        def _():
            forward(c, False)

        q_taken(c).wait_recv()

        @pl.when(c + 1 < steps)
        def _():
            q_give(c + 1).start()

        compute(c, 1 - b)
        x_give(c).start()

        @pl.when(c > 0)
        def _():
            relay(c - 1)

        q_keep(c).wait()
        compute(c, b)
        att_local(c).start()
        spread(True, b, c)

        @pl.when(c > 0)
        def _():
            att_forward(b, c - 1)

        @pl.when(c > 1)
        def _():
            att_forward(1 - b, c - 2)

    loop(step)
    relay(steps - 1)
    att_forward(1 - b, steps - 2)
    att_forward(b, steps - 1)
    att_forward(1 - b, steps - 1)

    def drain(c):
        for which in range(2):
            kv_give(c, which).wait_send()
        q_give(c).wait_send()
        x_give(c).wait_send()

        @pl.when(a < depth - 1)
        def _():
            for lag in range(depth):
                @pl.when(lag <= a)
                def _():
                    z_copy(c, a - lag).wait_send()

        att_local(c).wait()
        for own in (True, False):
            half = b if own else 1 - b
            att_core(own, half, c).wait_send()
            att_arrived(half, c, mate)
            for k in range(1, far):
                att_far(own, half, c, k).wait_send()
                att_fwd(half, c, k).wait_send()
                att_arrived(half, c, 2 * lax.rem(y + k, far) + 1 - core)

    loop(drain)
    pltpu.make_async_copy(wt_ref, wts_hbm.at[n], w_local).wait()
    for k in range(1, n_node):
        w_copy(k).wait_send()
        origin = lax.rem(n + k, n_node)
        remote(wt_ref, wts_hbm.at[origin], w_send.at[k], w_recv.at[origin], mate, s).wait_recv()


def attend(n_node, n_seq, q, wt, k, v):
    rows = q.shape[0]
    steps, far, depth = KEY_VALUE_HEADS // 2, n_node // 2, n_seq // 2
    dma = pltpu.SemaphoreType.DMA
    hbm = pl.BlockSpec(memory_space=pl.ANY)
    return pl.pallas_call(
        functools.partial(attend_kernel, n_node, n_seq, rows),
        out_shape=(
            jax.ShapeDtypeStruct((n_node,) + q.shape, jnp.bfloat16),
            jax.ShapeDtypeStruct((n_node,) + wt.shape, jnp.float32),
        ),
        in_specs=[pl.BlockSpec(memory_space=pltpu.VMEM), hbm, hbm, hbm],
        out_specs=(hbm, hbm),
        scratch_shapes=[
            pltpu.VMEM((steps, 2, n_seq * rows, HEAD_SIZE), jnp.bfloat16),
            pltpu.VMEM((steps, 2, rows, GROUP_COLS), jnp.bfloat16),
            pltpu.VMEM((steps, 2, rows, GROUP_COLS), jnp.bfloat16),
            dma((steps, 2)), dma((steps, 2)), dma((steps, 2)),
            dma((steps,)), dma((steps,)), dma((steps,)),
            dma((steps, depth)), dma((steps, depth)),
            dma((steps,)), dma((steps,)),
            dma((steps,)),
            dma((2, steps, n_node)),
            dma((2, steps)),
            dma((2, steps, far)),
            dma((2, steps, far)),
            dma,
            dma((n_node,)),
            dma((n_node,)),
        ],
        compiler_params=pltpu.CompilerParams(
            collective_id=0, has_side_effects=True, vmem_limit_bytes=60 * 1024 * 1024
        ),
    )(wt, q, k, v)


def pick_kernel(cap, att_ref, wt_ref, out_ref):
    rows, width = att_ref.shape[1:]
    first = EXP_NODE * lax.axis_index("node")
    earlier = lax.broadcasted_iota(jnp.int32, (rows, rows), 0) < lax.broadcasted_iota(
        jnp.int32, (rows, rows), 1
    )
    earlier = earlier.astype(jnp.float32).astype(jnp.bfloat16)
    slots = lax.broadcasted_iota(jnp.int32, (cap, rows), 0).astype(jnp.float32)
    for m in range(att_ref.shape[0]):
        tables = []
        for e in range(EXP_NODE):
            weight = jnp.broadcast_to(wt_ref[m, pl.ds(first + e, 1), :], (8, rows))
            member = jnp.where(weight > 0, jnp.float32(1.0), jnp.float32(0.0))
            rank = jnp.dot(member.astype(jnp.bfloat16), earlier, preferred_element_type=jnp.float32)
            gate = jnp.broadcast_to(weight[:1], (cap, rows))
            place = jnp.broadcast_to(rank[:1], (cap, rows))
            tables.append(jnp.where((gate > 0) & (place == slots), gate, 0.0).astype(jnp.bfloat16))
        table = jnp.concatenate(tables, axis=0)
        for at in range(0, width, 512):
            rows_out = jnp.dot(
                table, att_ref[m, :, at : at + 512], preferred_element_type=jnp.float32
            ).astype(jnp.bfloat16)
            for e in range(EXP_NODE):
                out_ref[e, 0, m, :, at : at + 512] = rows_out[e * cap : (e + 1) * cap]


def pick(cap, att, wts):
    n_node, rows, width = att.shape
    return pl.pallas_call(
        functools.partial(pick_kernel, cap),
        grid=(n_node // 2,),
        out_shape=jax.ShapeDtypeStruct((EXP_NODE, 1, n_node, cap, width), jnp.bfloat16),
        in_specs=[
            pl.BlockSpec((2, rows, width), lambda i: (i, 0, 0)),
            pl.BlockSpec((2,) + wts.shape[1:], lambda i: (i, 0, 0)),
        ],
        out_specs=pl.BlockSpec((EXP_NODE, 1, 2, cap, width), lambda i: (0, 0, i, 0, 0)),
        compiler_params=pltpu.CompilerParams(vmem_limit_bytes=60 * 1024 * 1024),
    )(att, wts)


def per_device(n_node, n_seq, queries, keys, values, routes, gates):
    experts = EXP_NODE * n_node
    cap = queries.shape[0] * TOP * 3 // (2 * experts)
    match = routes[None, :, :] == jnp.arange(experts, dtype=jnp.int32)[:, None, None]
    wt = jnp.sum(jnp.where(match, gates.astype(jnp.float32)[None], jnp.float32(0.0)), axis=2)
    att, wts = attend(n_node, n_seq, queries, wt, keys, values)
    return pick(cap, att, wts)


def solution(mesh):
    spec = P(("node", "seq"), None)
    return jax.shard_map(
        functools.partial(per_device, mesh.shape["node"], mesh.shape["seq"]),
        mesh=mesh,
        in_specs=(spec,) * 5,
        out_specs=P("node", "seq", None, None, None),
        check_vma=False,
    )
```
